256 devices in a mesh: seq: 32 (over x, y, core), dp: 8 (over z).
Axes of the slice: x: 4, y: 4, z: 8, core: 2. Of those that a mesh axis runs over, the one named last changes fastest.
Arguments:
- queries: bfloat16 [65536, 2048], P(('dp', 'seq')), parts along dimension 0, may hold values from -6 to 6
- keys: bfloat16 [65536, 2048], P(('dp', 'seq')), parts along dimension 0, may hold values from -6 to 6
- values: bfloat16 [65536, 2048], P(('dp', 'seq')), parts along dimension 0, may hold values from -6 to 6
- out_grad: bfloat16 [65536, 2048], P(('dp', 'seq')), parts along dimension 0, may hold values from -6 to 6
Outputs:
- attended: bfloat16 [65536, 2048], P(('dp', 'seq')), parts along dimension 0
- grad_query: bfloat16 [65536, 2048], P(('dp', 'seq')), parts along dimension 0
- grad_key: bfloat16 [65536, 2048], P(('dp', 'seq')), parts along dimension 0
- grad_value: bfloat16 [65536, 2048], P(('dp', 'seq')), parts along dimension 0
The draws below stay inside these ranges and needn't reach their ends.
There are 8 independent parts, one for each index of `dp`. The reference program is written for one: setup_inputs(seed, part) draws one part's arguments, and reference() takes and returns one part's arrays. A program takes and returns all parts, laid end to end along the dimension named above; each array names one. Nothing has to cross between parts.
All inputs are finite; a program needn't handle non-finite values.
Results may differ from the reference program's by a relative error of at most 0.0049.
Values sent between devices are 32-bit elements; how exact they have to be, the bound alone decides.
No kernel may reach another device: no remote copies, remote signals or barrier semaphores. Data moves between devices by JAX's collectives and lax.ppermute only.
A program may use at most 256 MiB of HBM per device.

```python
import jax
import jax.numpy as jnp
from jax import lax

HEADS = 16
DH = 128
TOK_DEV = 256
SEQ = 8192
WIDTH = 2048


def level_of(key, dims, cuts, smallest, top_value):
    level = 1.0
    for dim, parts in cuts:
        draws = jax.random.uniform(jax.random.fold_in(jax.random.fold_in(key, 6), dim), (parts,), jnp.float32, smallest / len(cuts), top_value / len(cuts))
        level = level * jnp.repeat(jnp.exp(draws), dims[dim] // parts).reshape((-1,) + (1,) * (len(dims) - 1 - dim))
    return level


def gaussian(stream_key, shape, scale, reach, shards=(), held_as=jnp.bfloat16):
    drawn = scale * jax.random.normal(stream_key, shape, jnp.float32)
    if shards:
        drawn = drawn * level_of(stream_key, shape, shards, -0.22, 0.18)
    return jnp.clip(drawn, -reach, reach).astype(held_as)


def setup_inputs(seed: int = 0, part: int = 0) -> dict:
    streams_of = jax.random.split(jax.random.key(seed), 5)
    part_keys = jax.random.split(jax.random.fold_in(streams_of[4], part), 5)
    return {
        "queries": gaussian(part_keys[0], (SEQ, WIDTH), 1.0, 6.0, ((0, 32),)),
        "keys": gaussian(part_keys[1], (SEQ, WIDTH), 1.0, 6.0, ((0, 32),)),
        "values": gaussian(part_keys[2], (SEQ, WIDTH), 1.0, 6.0, ((0, 32),)),
        "out_grad": gaussian(part_keys[3], (SEQ, WIDTH), 1.0, 6.0, ((0, 32),)),
    }


def per_head(blocks):
    query_b, key_b, value_b, grad_b = blocks
    factor = (DH * SEQ) ** -0.5
    causal = jnp.arange(TOK_DEV)[:, None] >= jnp.arange(TOK_DEV)[None, :]

    def weights_of(left, right):
        raw = jnp.dot(left, right.T, preferred_element_type=jnp.float32)
        return jnp.where(causal, factor * raw, jnp.float32(0.0)).astype(jnp.bfloat16)

    def forward_step(carry_state, block):
        query, key, value, grad = block
        state_bf = carry_state.astype(jnp.bfloat16)
        attn_w = weights_of(query, key)
        grad_w = weights_of(grad, value)
        output = (jnp.dot(attn_w, value, preferred_element_type=jnp.float32)
                  + jnp.dot(query, state_bf, preferred_element_type=jnp.float32)).astype(jnp.bfloat16)
        grad_q = (jnp.dot(grad_w, key, preferred_element_type=jnp.float32)
                  + jnp.dot(grad, state_bf.T, preferred_element_type=jnp.float32)).astype(jnp.bfloat16)
        new_state = carry_state + factor * jnp.dot(key.T, value, preferred_element_type=jnp.float32)
        return new_state, (output, grad_q)

    def backward_step(carry_state, block):
        query, key, value, grad = block
        state_bf = carry_state.astype(jnp.bfloat16)
        attn_w = weights_of(query, key)
        grad_w = weights_of(grad, value)
        grad_k = (jnp.dot(grad_w.T, query, preferred_element_type=jnp.float32)
                  + jnp.dot(value, state_bf.T, preferred_element_type=jnp.float32)).astype(jnp.bfloat16)
        grad_v = (jnp.dot(attn_w.T, grad, preferred_element_type=jnp.float32)
                  + jnp.dot(key, state_bf, preferred_element_type=jnp.float32)).astype(jnp.bfloat16)
        new_state = carry_state + factor * jnp.dot(query.T, grad, preferred_element_type=jnp.float32)
        return new_state, (grad_k, grad_v)

    start_state = jnp.zeros((DH, DH), jnp.float32)
    _, (output, grad_q) = lax.scan(forward_step, start_state, (query_b, key_b, value_b, grad_b))
    _, (grad_k, grad_v) = lax.scan(backward_step, start_state, (query_b, key_b, value_b, grad_b), reverse=True)
    return output, grad_q, grad_k, grad_v


def to_heads(array):
    blocks = SEQ // TOK_DEV
    return array.reshape(blocks, TOK_DEV, HEADS, DH).transpose(2, 0, 1, 3)


def from_heads(array):
    return array.transpose(1, 2, 0, 3).reshape(SEQ, HEADS * DH)


def reference(queries, keys, values, out_grad):
    output, grad_q, grad_k, grad_v = lax.map(
        per_head, (to_heads(queries), to_heads(keys), to_heads(values), to_heads(out_grad)))
    return (from_heads(output), from_heads(grad_q), from_heads(grad_k), from_heads(grad_v))
```

```python
import functools

import jax
import jax.numpy as jnp
from jax import lax
from jax.experimental import pallas as pl
from jax.experimental.pallas import tpu as pltpu
from jax.sharding import PartitionSpec as P

DH = 128
F32 = jnp.float32
BF16 = jnp.bfloat16
LEFT = (((0,), (0,)), ((), ()))
RIGHT = (((1,), (1,)), ((), ()))
PLAIN = (((1,), (0,)), ((), ()))
MIB = 1024 * 1024
PAIR = 2
COLS = PAIR * DH
HELD = 0
Q, G, K, V = range(4)

SMEM = pl.BlockSpec(memory_space=pltpu.SMEM)
VMEM = pl.BlockSpec(memory_space=pltpu.VMEM)
HBM = pl.BlockSpec(memory_space=pltpu.HBM)
ANY = pl.BlockSpec(memory_space=pl.ANY)


def dot(a, b, dims):
    return lax.dot_general(a, b, dims, preferred_element_type=F32)


def call(body, out_shape, in_specs, out_specs, scratch=(), flops=0, nbytes=0, name=None, limit=24, **kw):
    return pl.pallas_call(
        body,
        in_specs=in_specs,
        out_specs=out_specs,
        out_shape=out_shape,
        scratch_shapes=list(scratch),
        compiler_params=pltpu.CompilerParams(vmem_limit_bytes=limit * MIB),
        cost_estimate=pl.CostEstimate(flops=flops, bytes_accessed=nbytes, transcendentals=0),
        name=name,
        **kw,
    )


def hbm(x):
    return pltpu.with_memory_space_constraint(x, pltpu.HBM)


def vmem(x):
    return pltpu.with_memory_space_constraint(x, pltpu.VMEM)


def aligned(i, size):
    return pl.ds(pl.multiple_of(i * size, size), size)


def begin(src, dst, sem):
    copy = pltpu.make_async_copy(src, dst, sem)
    copy.start()
    return copy


def chunk_copies(i, side, srcs, buf, sems):
    chunks = buf.shape[2] // COLS
    return [
        pltpu.make_async_copy(src.at[:, aligned(side * chunks + i, COLS)], buf.at[a, :, aligned(i, COLS)], sems.at[a, i])
        for a, src in enumerate(srcs)
    ]


def own_states(factor, act, out, first, chunk):
    rows = out.shape[2]
    per = DH // rows
    for j in range(PAIR):
        cols = aligned(first + j, DH)
        owners = pl.ds((chunk * PAIR + j) * per, per)
        u = factor * dot(act[K, :, cols], act[V, :, cols], LEFT)
        w = factor * dot(act[Q, :, cols], act[G, :, cols], LEFT)
        out[owners, 0] = u.reshape(per, rows, DH)
        out[owners, 1] = w.reshape(per, rows, DH)


def send_body(factor, where, q, g, k, v, out, act, sems):
    chunks = q.shape[1] // 2 // COLS
    mine = where[0]

    def copies(h, i):
        cols = aligned(h * chunks + i, COLS)
        return [
            pltpu.make_async_copy(src.at[:, cols], act.at[a, :, cols], sems.at[a, h * chunks + i])
            for a, src in enumerate((q, g, k, v))
        ]

    for h in (1 - mine, mine):
        for i in range(chunks):
            for copy in copies(h, i):
                copy.start()

    @pl.loop(0, chunks)
    def _(i):
        for copy in copies(1 - mine, i):
            copy.wait()
        own_states(factor, act, out, ((1 - mine) * chunks + i) * PAIR, i)

    for i in range(chunks):
        for copy in copies(mine, i):
            copy.wait()


def send_states(where, acts, factor, owners, rows):
    tok, width = acts[0].shape
    return call(
        functools.partial(send_body, factor),
        [pltpu.VMEM((owners, 2, rows, DH), F32), pltpu.VMEM((4, tok, width), BF16)],
        [SMEM] + [HBM] * 4,
        [VMEM] * 2,
        [pltpu.SemaphoreType.DMA((4, width // COLS))],
        flops=2 * width * tok * DH,
        nbytes=8 * tok * width,
        name="send_states",
    )(where, *map(hbm, acts))


def keep_body(factor, where, act, out):
    chunks = act.shape[2] // 2 // COLS
    for i in range(chunks):
        own_states(factor, act, out, (where[0] * chunks + i) * PAIR, i)


def keep_states(where, act, factor, owners, rows):
    _, tok, width = act.shape
    return call(
        functools.partial(keep_body, factor),
        jax.ShapeDtypeStruct((owners, 2, rows, DH), F32),
        [SMEM, VMEM],
        VMEM,
        flops=2 * width * tok * DH,
        nbytes=4 * tok * width,
        name="keep_states",
    )(where, vmem(act))


def add_body(a, b, out, buf, sems):
    parts = sems.shape[0]
    size = buf.shape[0] // parts
    copies = []
    for i in range(parts):
        rows = pl.ds(i * size, size)
        buf[rows] = a[rows] + b[rows]
        copies.append(begin(buf.at[rows], out.at[rows], sems.at[i]))
    for copy in copies:
        copy.wait()


def add(a, b):
    return call(
        add_body,
        pltpu.HBM(a.shape, F32),
        [VMEM] * 2,
        HBM,
        [pltpu.VMEM(a.shape, F32), pltpu.SemaphoreType.DMA((4,))],
        flops=a.size,
        nbytes=12 * a.size,
        name="chip_states",
    )(a, b)


def scan_body(x, after, out, res, stores):
    n = x.shape[0]
    step = n // stores.shape[1]
    total = [jnp.zeros(x.shape[2:], F32)] * 2
    ends = []
    for i in range(n // step):
        for a in range(2):
            for j in range(i * step, (i + 1) * step):
                j = n - 1 - j if a else j
                res[j, a] = total[a]
                total[a] = total[a] + x[j, a]
            span = pl.ds(n - (i + 1) * step if a else i * step, step)
            ends.append(begin(res.at[span, a], out.at[span, a], stores.at[a, i]))
    for copy in ends:
        copy.wait()


def scan(x, after):
    return call(
        scan_body,
        pltpu.HBM(x.shape, F32),
        [VMEM, HBM],
        HBM,
        [pltpu.VMEM(x.shape, F32), pltpu.SemaphoreType.DMA((2, 4))],
        flops=x.size,
        nbytes=8 * x.size,
        name="scan",
    )(x, hbm(after))


def local_body(factor, where, before, near, kept, q, g, k, v, out, give, act, ext, res, loads, eload, stores):
    tok = q.shape[0]
    chunks = act.shape[2] // COLS
    other = 1 - where[0]
    flags = (1.0 - other.astype(F32), other.astype(F32))
    extra = begin(near if kept is None else near.at[:, other], ext, eload.at[0])
    if kept is not None:
        passed = begin(kept.at[:, where[0]], give, eload.at[1])
    copies = lambda i: chunk_copies(i, where[1], (q, g, k, v), act, loads)
    for i in range(chunks):
        for copy in copies(i):
            copy.start()
    causal = lax.broadcasted_iota(jnp.int32, (tok, tok), 0) >= lax.broadcasted_iota(
        jnp.int32, (tok, tok), 1
    )
    extra.wait()
    per = ext.shape[0] // (chunks * PAIR)

    def store(i):
        cols = aligned(i, COLS)
        return pltpu.make_async_copy(res.at[:, :, cols], out.at[:, :, cols], stores.at[i])

    @pl.loop(0, chunks)
    def _(i):
        for copy in copies(i):
            copy.wait()
        for j in range(PAIR):
            head = i * PAIR + j
            cols = aligned(head, DH)
            qh, gh, kh, vh = (act[a, :, cols] for a in range(4))
            p = jnp.where(causal, factor * dot(qh, kh, RIGHT), 0.0).astype(BF16)
            e = jnp.where(causal, factor * dot(gh, vh, RIGHT), 0.0).astype(BF16)
            s = ext[pl.ds(head * per, per)].reshape(DH, DH).astype(BF16)
            plain = dot(act[2 * other, :, cols], s, PLAIN)
            turned = dot(act[2 * other + 1, :, cols], s, RIGHT)
            res[Q, :, cols] = (dot(p, vh, PLAIN) + flags[0] * plain).astype(BF16)
            res[G, :, cols] = (dot(e, kh, PLAIN) + flags[0] * turned).astype(BF16)
            res[K, :, cols] = (dot(p, gh, LEFT) + flags[1] * plain).astype(BF16)
            res[V, :, cols] = (dot(e, qh, LEFT) + flags[1] * turned).astype(BF16)
        store(i).start()

    for i in range(chunks):
        store(i).wait()
    if kept is not None:
        passed.wait()


def local_rest(factor, where, before, near, q, g, k, v, out, *scratch):
    local_body(factor, where, before, near, None, q, g, k, v, out, None, *scratch)


def local(where, before, near, acts, factor, kept=None):
    tok, width = acts[0].shape
    chunks = width // COLS // 2
    half = pltpu.VMEM((4, tok, width // 2), BF16)
    shape = near.shape[:1] + near.shape[-2:]
    out = pltpu.HBM((4, tok, width // 2), BF16)
    first = kept is not None
    return call(
        functools.partial(local_body if first else local_rest, factor),
        [out, pltpu.HBM(shape, F32)] if first else out,
        [SMEM, HBM, ANY] + [ANY] * first + [HBM] * 4,
        [HBM] * 2 if first else HBM,
        [
            half,
            pltpu.VMEM(shape, F32),
            half,
            pltpu.SemaphoreType.DMA((4, chunks)),
            pltpu.SemaphoreType.DMA((2,)),
            pltpu.SemaphoreType.DMA((chunks,)),
        ],
        flops=8 * tok * tok * width,
        nbytes=tok * width * 12,
        name="local",
    )(where, hbm(before), near, *([kept] if first else []), *map(hbm, acts))


def order_body(z, loc, out):
    pass


def order(z, loc):
    out = jax.ShapeDtypeStruct(z.shape, F32)
    return call(order_body, out, [ANY] * 2, ANY, name="order", input_output_aliases={0: 0})(z, hbm(loc))


def finish_body(where, z, loc, q, g, k, v, *rest):
    outs, (zbuf, abuf, lbuf, obuf, zsem, asem, lsem, osem) = rest[-12:-8], rest[-8:]
    side = where[1]
    chunks = obuf.shape[2] // COLS
    size = z.shape[0] // chunks
    per = size // PAIR

    def loads(i):
        rows = pl.ds(i * size, size)
        cols = aligned(i, COLS)
        return [
            pltpu.make_async_copy(z.at[rows], zbuf.at[rows], zsem.at[i]),
            *chunk_copies(i, side, (q, g, k, v)[HELD:], abuf, asem),
        ]

    def stores(i):
        return [
            pltpu.make_async_copy(
                obuf.at[a, :, aligned(i, COLS)], out.at[:, aligned(side * chunks + i, COLS)], osem.at[a, i]
            )
            for a, out in enumerate(outs)
        ]

    for i in range(chunks):
        for copy in loads(i):
            copy.start()

    @pl.loop(0, chunks)
    def _(i):
        for copy in loads(i):
            copy.wait()

        for j in range(PAIR):
            head = i * PAIR + j
            cols = aligned(head, DH)
            whole = aligned(side * chunks * PAIR + head, DH)
            acts = [a[:, whole] for a in (q, g, k, v)[:HELD]] + [abuf[a, :, cols] for a in range(4 - HELD)]
            owners = pl.ds(head * per, per)
            s = zbuf[owners, 0].reshape(DH, DH).astype(BF16)
            r = zbuf[owners, 1].reshape(DH, DH).astype(BF16)
            for a, (state, dims) in enumerate(((s, PLAIN), (s, RIGHT), (r, PLAIN), (r, RIGHT))):
                obuf[a, :, cols] = (loc[a, :, cols] + dot(acts[a], state, dims)).astype(BF16)
        for copy in stores(i):
            copy.start()

    for i in range(chunks):
        for copy in stores(i):
            copy.wait()


def finish(where, z, acts, loc, outs=None):
    tok, width = acts[0].shape
    chunks = width // 2 // COLS
    args = [where, z, loc, *acts[:HELD], *map(hbm, acts[HELD:])]
    specs = [SMEM, ANY, VMEM] + [VMEM] * HELD + [HBM] * (4 - HELD)
    aliases = {}
    if outs is not None:
        aliases = {len(args) + i: i for i in range(4)}
        args += map(hbm, outs)
        specs += [HBM] * 4
    half = pltpu.VMEM((4, tok, width // 2), BF16)
    sems = pltpu.SemaphoreType.DMA((4, chunks))
    one = pltpu.SemaphoreType.DMA((chunks,))
    return call(
        finish_body,
        [pltpu.HBM((tok, width), BF16)] * 4,
        specs,
        [HBM] * 4,
        [pltpu.VMEM(z.shape, F32), half, half, half, one, sems, one, sems],
        flops=4 * tok * DH * width,
        nbytes=tok * width * 16,
        name="finish",
        input_output_aliases=aliases,
    )(*args)


def per_device(q, k, v, g):
    tok, width = q.shape
    acts = (q, g, k, v)
    n = lax.axis_size("seq")
    chips = n // 2
    rows = width // 2 // chips
    factor = float(DH * tok * n) ** (-0.5)
    core = (lax.axis_index("seq") % 2).astype(jnp.int32)
    mine = jnp.stack([core, core])
    other = jnp.stack([core, 1 - core])
    swap = [(i, i ^ 1) for i in range(n)]
    same_core = [list(range(c, n, 2)) for c in range(2)]

    def to_owner(t):
        return lax.all_to_all(t, "seq", 0, 0, axis_index_groups=same_core, tiled=True)

    sent, act = send_states(mine, acts, factor, chips, rows)
    received = lax.ppermute(sent, "seq", swap)
    kept = keep_states(mine, act, factor, chips, rows)
    chip = add(kept, received)
    at_owner = to_owner(chip)
    loc_mine, give = local(mine, chip, received, acts, factor, kept)
    earlier = scan(at_owner, loc_mine)
    far = lax.ppermute(give, "seq", swap)
    loc_other = local(other, earlier, far, acts, factor)
    z = order(to_owner(earlier), loc_other)
    zs = lax.ppermute(z, "seq", swap)
    outs = finish(mine, z, acts, loc_mine)
    o, gq, gv, gk = finish(other, zs, acts, loc_other, outs)
    return o, gq, gk, gv


def solution(mesh):
    placed = P(("dp", "seq"), None)
    return jax.shard_map(
        per_device,
        mesh=mesh,
        in_specs=(placed,) * 4,
        out_specs=(placed,) * 4,
        check_vma=False,
    )
```

```python
import functools

import jax
import jax.numpy as jnp
from jax import lax
from jax.experimental import pallas as pl
from jax.experimental.pallas import tpu as pltpu
from jax.sharding import PartitionSpec as P

DH = 128
F32 = jnp.float32
BF16 = jnp.bfloat16
LEFT = (((0,), (0,)), ((), ()))
RIGHT = (((1,), (1,)), ((), ()))
PLAIN = (((1,), (0,)), ((), ()))
MIB = 1024 * 1024
SIDE = 4
PAIR = 2
COLS = PAIR * DH
Q, G, K, V = range(4)

VMEM = pl.BlockSpec(memory_space=pltpu.VMEM)
HBM = pl.BlockSpec(memory_space=pltpu.HBM)
ANY = pl.BlockSpec(memory_space=pl.ANY)


def dot(a, b, dims):
    return lax.dot_general(a, b, dims, preferred_element_type=F32)


def call(body, out_shape, in_specs, out_specs, scratch=(), flops=0, nbytes=0, name=None, limit=8, **kw):
    return pl.pallas_call(
        body,
        in_specs=in_specs,
        out_specs=out_specs,
        out_shape=out_shape,
        scratch_shapes=list(scratch),
        compiler_params=pltpu.CompilerParams(vmem_limit_bytes=limit * MIB),
        cost_estimate=pl.CostEstimate(flops=flops, bytes_accessed=nbytes, transcendentals=0),
        name=name,
        **kw,
    )


def hbm(x):
    return pltpu.with_memory_space_constraint(x, pltpu.HBM)


def aligned(i, size):
    return pl.ds(pl.multiple_of(i * size, size), size)


def ring(i):
    return lax.rem(i + 2 * SIDE, SIDE)


def position():
    index = lax.axis_index("seq")
    return lax.rem(index, 2), lax.div(index, 2 * SIDE), lax.rem(lax.div(index, 2), SIDE)


def own_states(factor, act, out, side, i):
    for j in range(PAIR):
        cols = aligned((side * SIDE + i) * PAIR + j, DH)
        rows = pl.ds(j * DH, DH)
        out[i, 0, rows] = factor * dot(act[K, :, cols], act[V, :, cols], LEFT)
        out[i, 1, rows] = factor * dot(act[Q, :, cols], act[G, :, cols], LEFT)


def send_body(factor, q, g, k, v, out, act, sems):
    mine = position()[0]

    def copies(h, i):
        cols = aligned(h * SIDE + i, COLS)
        return [
            pltpu.make_async_copy(src.at[:, cols], act.at[a, :, cols], sems.at[a, h * SIDE + i])
            for a, src in enumerate((q, g, k, v))
        ]

    for h in (1 - mine, mine):
        for i in range(SIDE):
            for copy in copies(h, i):
                copy.start()

    @pl.loop(0, SIDE)
    def _(i):
        for copy in copies(1 - mine, i):
            copy.wait()
        own_states(factor, act, out, 1 - mine, i)

    for i in range(SIDE):
        for copy in copies(mine, i):
            copy.wait()


def send_states(acts, factor):
    tok, width = acts[0].shape
    return call(
        functools.partial(send_body, factor),
        [jax.ShapeDtypeStruct((SIDE, 2, COLS, DH), F32), jax.ShapeDtypeStruct((4, tok, width), BF16)],
        [HBM] * 4,
        [VMEM] * 2,
        [pltpu.SemaphoreType.DMA((4, width // COLS))],
        flops=2 * width * tok * DH,
        nbytes=8 * tok * width,
        name="send_states",
    )(*map(hbm, acts))


def keep_body(factor, act, out):
    mine = position()[0]
    for i in range(SIDE):
        own_states(factor, act, out, mine, i)


def keep_states(act, factor):
    _, tok, width = act.shape
    return call(
        functools.partial(keep_body, factor),
        jax.ShapeDtypeStruct((SIDE, 2, COLS, DH), F32),
        [VMEM],
        VMEM,
        flops=2 * width * tok * DH,
        nbytes=4 * tok * width,
        name="keep_states",
    )(act)


def chip_body(kept, received, *outs):
    _, _, y = position()
    for d, out in enumerate(outs):
        s = ring(y + d)
        out[...] = kept[s] + received[s]


def chip_states(kept, received):
    return call(
        chip_body,
        [jax.ShapeDtypeStruct(kept.shape[1:], F32)] * SIDE,
        [VMEM] * 2,
        [VMEM] * SIDE,
        flops=kept.size,
        nbytes=kept.size * 12,
        name="chip_states",
    )(kept, received)


def row_body(after, *refs):
    _, x, y = position()
    pieces, (pre, *outs), buf = refs[:SIDE], refs[SIDE:-1], refs[-1]
    for d, piece in enumerate(pieces):
        buf[ring(y - d)] = piece[...]
    ahead = jnp.zeros(buf.shape[2:], F32)
    behind = ahead
    for s in range(SIDE):
        pre[s, 0] = ahead
        ahead = ahead + buf[s, 0]
    for s in range(SIDE - 1, -1, -1):
        pre[s, 1] = behind
        behind = behind + buf[s, 1]
    for d, out in enumerate(outs, 1):
        out[...] = jnp.where(x + d < SIDE, ahead, behind)


def row_states(after, pieces):
    shape = pieces[0].shape
    return call(
        row_body,
        [jax.ShapeDtypeStruct((SIDE,) + shape, F32)] + [jax.ShapeDtypeStruct(shape[1:], F32)] * (SIDE - 1),
        [ANY] + [VMEM] * SIDE,
        [VMEM] * SIDE,
        [pltpu.VMEM((SIDE,) + shape, F32)],
        flops=8 * pieces[0].size,
        nbytes=40 * pieces[0].size,
        name="row_states",
    )(after, *pieces)


def all_body(pre, *refs):
    _, x, y = position()
    totals, outs = refs[: SIDE - 1], refs[SIDE - 1 :]
    ahead = jnp.zeros(totals[0].shape, F32)
    behind = ahead
    for d, total in enumerate(totals, 1):
        lower = x >= d
        ahead = ahead + jnp.where(lower, total[...], 0.0)
        behind = behind + jnp.where(lower, 0.0, total[...])
    for d, out in enumerate(outs):
        s = ring(y + d)
        out[0] = pre[s, 0] + ahead
        out[1] = pre[s, 1] + behind


def all_states(pre, totals):
    return call(
        all_body,
        [jax.ShapeDtypeStruct(pre.shape[1:], F32)] * SIDE,
        [VMEM] * SIDE,
        [VMEM] * SIDE,
        flops=2 * pre.size,
        nbytes=10 * pre.size,
        name="all_states",
    )(pre, *totals)


def gather_body(after, *refs):
    core, _, y = position()
    pieces, (kept, received, mine, send) = refs[:SIDE], refs[SIDE:]
    second = core.astype(F32)
    first = 1.0 - second
    for d, piece in enumerate(pieces):
        s = ring(y - d)
        send[s, 0] = piece[0] + first * kept[s, 0]
        send[s, 1] = piece[1] + second * kept[s, 1]
        mine[s, 0] = (piece[0] + second * received[s, 0]).astype(BF16)
        mine[s, 1] = (piece[1] + first * received[s, 1]).astype(BF16)


def gather_states(after, pieces, kept, received):
    return call(
        gather_body,
        [jax.ShapeDtypeStruct(kept.shape, BF16), jax.ShapeDtypeStruct(kept.shape, F32)],
        [ANY] + [VMEM] * (SIDE + 2),
        [VMEM] * 2,
        flops=4 * kept.size,
        nbytes=22 * kept.size,
        name="gather_states",
    )(after, *pieces, kept, received)


def local_body(factor, first, count, after, act, *rest):
    out, tail = rest[-2:]
    tok = act.shape[1]
    causal = lax.broadcasted_iota(jnp.int32, (tok, tok), 0) >= lax.broadcasted_iota(
        jnp.int32, (tok, tok), 1
    )

    @pl.loop(first // PAIR, (first + count) // PAIR)
    def _(i):
        for j in range(PAIR):
            cols = aligned(i * PAIR + j, DH)
            qh, gh, kh, vh = (act[a, :, cols] for a in range(4))
            p = jnp.where(causal, factor * dot(qh, kh, RIGHT), 0.0).astype(BF16)
            e = jnp.where(causal, factor * dot(gh, vh, RIGHT), 0.0).astype(BF16)
            out[Q, :, cols] = dot(p, vh, PLAIN)
            out[G, :, cols] = dot(e, kh, PLAIN)
            out[K, :, cols] = dot(p, gh, LEFT)
            out[V, :, cols] = dot(e, qh, LEFT)

    tail[...] = jnp.zeros(tail.shape, F32)


def local(after, act, factor, first, count, loc=None):
    _, tok, width = act.shape
    args = [after, act]
    aliases = {}
    if loc is not None:
        args.append(loc)
        aliases = {2: 0}
    return call(
        functools.partial(local_body, factor, first, count),
        [jax.ShapeDtypeStruct((4, tok, width), F32), jax.ShapeDtypeStruct((8, DH), F32)],
        [ANY] + [VMEM] * (len(args) - 1),
        [VMEM] * 2,
        flops=12 * tok * tok * DH * count,
        nbytes=tok * width * 12,
        name="local",
        input_output_aliases=aliases,
    )(*args)


def finish_body(own, state, act, loc, *rest):
    outs, (obuf, sems) = rest[-6:-2], rest[-2:]
    core = position()[0]
    side = core if own else 1 - core

    def stores(i):
        return [
            pltpu.make_async_copy(
                obuf.at[a, :, aligned(i, COLS)], out.at[:, aligned(side * SIDE + i, COLS)], sems.at[a, i]
            )
            for a, out in enumerate(outs)
        ]

    @pl.loop(0, SIDE)
    def _(i):
        for j in range(PAIR):
            cols = aligned((side * SIDE + i) * PAIR + j, DH)
            here = aligned(i * PAIR + j, DH)
            rows = pl.ds(j * DH, DH)
            s = state[i, 0, rows].astype(BF16)
            r = state[i, 1, rows].astype(BF16)
            for a, (m, dims) in enumerate(((s, PLAIN), (s, RIGHT), (r, PLAIN), (r, RIGHT))):
                obuf[a, :, here] = (loc[a, :, cols] + dot(act[a, :, cols], m, dims)).astype(BF16)
        for copy in stores(i):
            copy.start()

    for i in range(SIDE):
        for copy in stores(i):
            copy.wait()


def finish(state, act, loc, outs=None):
    _, tok, width = act.shape
    args = [state, act, loc]
    specs = [VMEM] * 3
    aliases = {}
    if outs is not None:
        aliases = {len(args) + i: i for i in range(4)}
        args += map(hbm, outs)
        specs += [HBM] * 4
    return call(
        functools.partial(finish_body, outs is None),
        [pltpu.HBM((tok, width), BF16)] * 4,
        specs,
        [HBM] * 4,
        [pltpu.VMEM((4, tok, width // 2), BF16), pltpu.SemaphoreType.DMA((4, SIDE))],
        flops=4 * tok * DH * width,
        nbytes=tok * width * 16,
        name="finish",
        input_output_aliases=aliases,
    )(*args)


def per_device(q, k, v, g):
    tok, width = q.shape
    heads = width // DH
    n = lax.axis_size("seq")
    factor = float(DH * tok * n) ** (-0.5)
    def to_sibling(t):
        return lax.ppermute(t, "seq", [(i, i ^ 1) for i in range(n)])

    def along_x(t, d):
        return lax.ppermute(t, "seq", [(i, (i + d * 2 * SIDE) % n) for i in range(n)])

    def along_y(t, d):
        row = 2 * SIDE
        return lax.ppermute(t, "seq", [(i, i // row * row + (i + 2 * d) % row) for i in range(n)])

    sent, act = send_states((q, g, k, v), factor)
    received = to_sibling(sent)
    kept = keep_states(act, factor)
    pieces = chip_states(kept, received)
    gathered = [pieces[0]] + [along_y(pieces[d], d) for d in range(1, SIDE)]
    loc, after = local(pieces[0], act, factor, 0, heads // 2)
    pre, *totals = row_states(after, gathered)
    totals = [along_x(t, d) for d, t in enumerate(totals, 1)]
    pieces = all_states(pre, totals)
    back = [pieces[0]] + [along_y(pieces[d], d) for d in range(1, SIDE)]
    loc, after = local(pieces[0], act, factor, heads // 2, heads // 2, loc)
    state, send = gather_states(after, back, kept, received)
    got = to_sibling(send)
    outs = finish(state, act, loc)
    o, gq, gv, gk = finish(got, act, loc, outs)
    return o, gq, gk, gv


def solution(mesh):
    placed = P(("dp", "seq"), None)
    return jax.shard_map(
        per_device,
        mesh=mesh,
        in_specs=(placed,) * 4,
        out_specs=(placed,) * 4,
        check_vma=False,
    )
```

```python
import functools

import jax
import jax.numpy as jnp
from jax import lax
from jax.experimental import pallas as pl
from jax.experimental.pallas import tpu as pltpu
from jax.sharding import PartitionSpec as P

DH = 128
F32 = jnp.float32
BF16 = jnp.bfloat16
LEFT = (((0,), (0,)), ((), ()))
RIGHT = (((1,), (1,)), ((), ()))
PLAIN = (((1,), (0,)), ((), ()))
MIB = 1024 * 1024
SIDE = 4
PAIR = 2
COLS = PAIR * DH
Q, G, K, V = range(4)

VMEM = pl.BlockSpec(memory_space=pltpu.VMEM)
HBM = pl.BlockSpec(memory_space=pltpu.HBM)
ANY = pl.BlockSpec(memory_space=pl.ANY)


def dot(a, b, dims):
    return lax.dot_general(a, b, dims, preferred_element_type=F32)


def call(body, out_shape, in_specs, out_specs, scratch=(), flops=0, nbytes=0, name=None, limit=8, **kw):
    return pl.pallas_call(
        body,
        in_specs=in_specs,
        out_specs=out_specs,
        out_shape=out_shape,
        scratch_shapes=list(scratch),
        compiler_params=pltpu.CompilerParams(vmem_limit_bytes=limit * MIB),
        cost_estimate=pl.CostEstimate(flops=flops, bytes_accessed=nbytes, transcendentals=0),
        name=name,
        **kw,
    )


def hbm(x):
    return pltpu.with_memory_space_constraint(x, pltpu.HBM)


def aligned(i, size):
    return pl.ds(pl.multiple_of(i * size, size), size)


def ring(i):
    return lax.rem(i + 2 * SIDE, SIDE)


def position():
    index = lax.axis_index("seq")
    return lax.rem(index, 2), lax.div(index, 2 * SIDE), lax.rem(lax.div(index, 2), SIDE)


def own_states(factor, act, outs, side, i):
    for j, out in enumerate(outs):
        cols = aligned((side * SIDE + i) * PAIR + j, DH)
        out[i, 0] = factor * dot(act[K, :, cols], act[V, :, cols], LEFT)
        out[i, 1] = factor * dot(act[Q, :, cols], act[G, :, cols], LEFT)


def send_body(factor, q, g, k, v, *rest):
    outs, (act, sems) = rest[:PAIR], rest[PAIR:]
    mine = position()[0]

    def copies(h, i):
        cols = aligned(h * SIDE + i, COLS)
        return [
            pltpu.make_async_copy(src.at[:, cols], act.at[a, :, cols], sems.at[a, h * SIDE + i])
            for a, src in enumerate((q, g, k, v))
        ]

    for h in (1 - mine, mine):
        for i in range(SIDE):
            for copy in copies(h, i):
                copy.start()

    @pl.loop(0, SIDE)
    def _(i):
        for copy in copies(1 - mine, i):
            copy.wait()
        own_states(factor, act, outs, 1 - mine, i)

    for i in range(SIDE):
        for copy in copies(mine, i):
            copy.wait()


def send_states(acts, factor):
    tok, width = acts[0].shape
    return call(
        functools.partial(send_body, factor),
        [jax.ShapeDtypeStruct((SIDE, 2, DH, DH), F32)] * PAIR + [jax.ShapeDtypeStruct((4, tok, width), BF16)],
        [HBM] * 4,
        [VMEM] * (PAIR + 1),
        [pltpu.SemaphoreType.DMA((4, width // COLS))],
        flops=2 * width * tok * DH,
        nbytes=8 * tok * width,
        name="send_states",
    )(*map(hbm, acts))


def keep_body(factor, act, *outs):
    mine = position()[0]
    for i in range(SIDE):
        own_states(factor, act, outs, mine, i)


def keep_states(act, factor):
    _, tok, width = act.shape
    return call(
        functools.partial(keep_body, factor),
        [jax.ShapeDtypeStruct((SIDE, 2, DH, DH), F32)] * PAIR,
        [VMEM],
        [VMEM] * PAIR,
        flops=2 * width * tok * DH,
        nbytes=4 * tok * width,
        name="keep_states",
    )(act)


def chip_body(kept, received, *outs):
    _, _, y = position()
    for d, out in enumerate(outs):
        s = ring(y + d)
        out[...] = kept[s] + received[s]


def chip_states(kept, received):
    return call(
        chip_body,
        [jax.ShapeDtypeStruct(kept.shape[1:], F32)] * SIDE,
        [VMEM] * 2,
        [VMEM] * SIDE,
        flops=kept.size,
        nbytes=kept.size * 12,
        name="chip_states",
    )(kept, received)


def row_body(after, *refs):
    _, x, y = position()
    pieces, (pre, *outs), buf = refs[:SIDE], refs[SIDE:-1], refs[-1]
    for d, piece in enumerate(pieces):
        buf[ring(y - d)] = piece[...]
    ahead = jnp.zeros(buf.shape[2:], F32)
    behind = ahead
    for s in range(SIDE):
        pre[s, 0] = ahead
        ahead = ahead + buf[s, 0]
    for s in range(SIDE - 1, -1, -1):
        pre[s, 1] = behind
        behind = behind + buf[s, 1]
    for d, out in enumerate(outs, 1):
        out[...] = jnp.where(x + d < SIDE, ahead, behind)


def row_states(after, pieces):
    shape = pieces[0].shape
    return call(
        row_body,
        [jax.ShapeDtypeStruct((SIDE,) + shape, F32)] + [jax.ShapeDtypeStruct(shape[1:], F32)] * (SIDE - 1),
        [ANY] + [VMEM] * SIDE,
        [VMEM] * SIDE,
        [pltpu.VMEM((SIDE,) + shape, F32)],
        flops=8 * pieces[0].size,
        nbytes=40 * pieces[0].size,
        name="row_states",
    )(after, *pieces)


def all_body(after, pre, *refs):
    _, x, y = position()
    totals, outs = refs[: SIDE - 1], refs[SIDE - 1 :]
    ahead = jnp.zeros(totals[0].shape, F32)
    behind = ahead
    for d, total in enumerate(totals, 1):
        lower = x >= d
        ahead = ahead + jnp.where(lower, total[...], 0.0)
        behind = behind + jnp.where(lower, 0.0, total[...])
    for d, out in enumerate(outs):
        s = ring(y + d)
        out[0] = pre[s, 0] + ahead
        out[1] = pre[s, 1] + behind


def all_states(after, pre, totals):
    return call(
        all_body,
        [jax.ShapeDtypeStruct(pre.shape[1:], F32)] * SIDE,
        [ANY] + [VMEM] * SIDE,
        [VMEM] * SIDE,
        flops=2 * pre.size,
        nbytes=10 * pre.size,
        name="all_states",
    )(after, pre, *totals)


def gather_body(after, *refs):
    core, _, y = position()
    pieces, (kept, received, mine, send) = refs[:SIDE], refs[SIDE:]
    second = core.astype(F32)
    first = 1.0 - second
    for d, piece in enumerate(pieces):
        s = ring(y - d)
        send[s, 0] = piece[0] + first * kept[s, 0]
        send[s, 1] = piece[1] + second * kept[s, 1]
        mine[s, 0] = (piece[0] + second * received[s, 0]).astype(BF16)
        mine[s, 1] = (piece[1] + first * received[s, 1]).astype(BF16)


def gather_states(after, pieces, kept, received):
    return call(
        gather_body,
        [jax.ShapeDtypeStruct(kept.shape, BF16), jax.ShapeDtypeStruct(kept.shape, F32)],
        [ANY] + [VMEM] * (SIDE + 2),
        [VMEM] * 2,
        flops=4 * kept.size,
        nbytes=22 * kept.size,
        name="gather_states",
    )(after, *pieces, kept, received)


def local_body(factor, part, side, after, act, *rest):
    out, tail = rest[-2:]
    tok = act.shape[1]
    causal = lax.broadcasted_iota(jnp.int32, (tok, tok), 0) >= lax.broadcasted_iota(
        jnp.int32, (tok, tok), 1
    )

    @pl.loop(side * SIDE, (side + 1) * SIDE, step=2)
    def _(first):
        for j in range(2):
            cols = aligned((first + j) * PAIR + part, DH)
            here = aligned(first + j, DH)
            qh, gh, kh, vh = (act[a, :, cols] for a in range(4))
            p = jnp.where(causal, factor * dot(qh, kh, RIGHT), 0.0).astype(BF16)
            e = jnp.where(causal, factor * dot(gh, vh, RIGHT), 0.0).astype(BF16)
            out[Q, :, here] = dot(p, vh, PLAIN)
            out[G, :, here] = dot(e, kh, PLAIN)
            out[K, :, here] = dot(p, gh, LEFT)
            out[V, :, here] = dot(e, qh, LEFT)

    tail[...] = jnp.zeros(tail.shape, F32)


def local(after, act, factor, part, side, loc=None):
    _, tok, width = act.shape
    args = [after, act]
    aliases = {}
    if loc is not None:
        args.append(loc)
        aliases = {2: 0}
    return call(
        functools.partial(local_body, factor, part, side),
        [jax.ShapeDtypeStruct((4, tok, width // PAIR), F32), jax.ShapeDtypeStruct((8, DH), F32)],
        [ANY] + [VMEM] * (len(args) - 1),
        [VMEM] * 2,
        flops=3 * tok * tok * width,
        nbytes=tok * width * 3,
        name="local",
        input_output_aliases=aliases,
    )(*args)


def finish_body(part, own, state, act, loc, *rest):
    outs, (obuf, sems) = rest[-6:-2], rest[-2:]
    core = position()[0]
    side = core if own else 1 - core

    def stores(i):
        cols = aligned((side * SIDE + i) * PAIR + part, DH)
        return [
            pltpu.make_async_copy(obuf.at[a, i], out.at[:, cols], sems.at[a, i]) for a, out in enumerate(outs)
        ]

    for i in range(SIDE):
        cols = aligned((side * SIDE + i) * PAIR + part, DH)
        here = aligned(side * SIDE + i, DH)
        s = state[i, 0].astype(BF16)
        r = state[i, 1].astype(BF16)
        for a, (m, dims) in enumerate(((s, PLAIN), (s, RIGHT), (r, PLAIN), (r, RIGHT))):
            obuf[a, i] = (loc[a, :, here] + dot(act[a, :, cols], m, dims)).astype(BF16)
        for copy in stores(i):
            copy.start()
    for i in range(SIDE):
        for copy in stores(i):
            copy.wait()


def finish(part, own, state, act, loc, outs):
    _, tok, width = act.shape
    args = [state, act, loc]
    specs = [VMEM] * 3
    aliases = {}
    if outs is not None:
        aliases = {len(args) + i: i for i in range(4)}
        args += map(hbm, outs)
        specs += [HBM] * 4
    return call(
        functools.partial(finish_body, part, own),
        [pltpu.HBM((tok, width), BF16)] * 4,
        specs,
        [HBM] * 4,
        [pltpu.VMEM((4, SIDE, tok, DH), BF16), pltpu.SemaphoreType.DMA((4, SIDE))],
        flops=2 * tok * DH * width,
        nbytes=tok * width * 8,
        name="finish",
        input_output_aliases=aliases,
    )(*args)


def per_device(q, k, v, g):
    tok, width = q.shape
    heads = width // DH
    n = lax.axis_size("seq")
    factor = float(DH * tok * n) ** (-0.5)
    def to_sibling(t):
        return lax.ppermute(t, "seq", [(i, i ^ 1) for i in range(n)])

    def along_x(t, d):
        return lax.ppermute(t, "seq", [(i, (i + d * 2 * SIDE) % n) for i in range(n)])

    def along_y(t, d):
        row = 2 * SIDE
        return lax.ppermute(t, "seq", [(i, i // row * row + (i + 2 * d) % row) for i in range(n)])

    def gather(pieces):
        return [pieces[0]] + [along_y(pieces[d], d) for d in range(1, SIDE)]

    parts = range(PAIR)
    *sent, act = send_states((q, g, k, v), factor)
    received = [to_sibling(t) for t in sent]
    kept = keep_states(act, factor)
    chip = [chip_states(kept[p], received[p]) for p in parts]
    gathered = [gather(t) for t in chip]
    loc0, after = local(chip[1][0], act, factor, 0, 0)
    pre0, *totals0 = row_states(after, gathered[0])
    totals0 = [along_x(t, d) for d, t in enumerate(totals0, 1)]
    loc0, after = local(pre0, act, factor, 0, 1, loc0)
    pre1, *totals1 = row_states(after, gathered[1])
    totals1 = [along_x(t, d) for d, t in enumerate(totals1, 1)]
    all0 = all_states(after, pre0, totals0)
    back0 = gather(all0)
    loc1, after = local(all0[0], act, factor, 1, 0)
    all1 = all_states(after, pre1, totals1)
    back1 = gather(all1)
    state0, send0 = gather_states(after, back0, kept[0], received[0])
    got0 = to_sibling(send0)
    loc1, after = local(all1[0], act, factor, 1, 1, loc1)
    outs = finish(0, True, state0, act, loc0, None)
    outs = finish(0, False, got0, act, loc0, outs)
    state1, send1 = gather_states(after, back1, kept[1], received[1])
    got1 = to_sibling(send1)
    outs = finish(1, True, state1, act, loc1, outs)
    o, gq, gv, gk = finish(1, False, got1, act, loc1, outs)
    return o, gq, gk, gv


def solution(mesh):
    placed = P(("dp", "seq"), None)
    return jax.shard_map(
        per_device,
        mesh=mesh,
        in_specs=(placed,) * 4,
        out_specs=(placed,) * 4,
        check_vma=False,
    )
```

```python
import functools

import jax
import jax.numpy as jnp
from jax import lax
from jax.experimental import pallas as pl
from jax.experimental.pallas import tpu as pltpu
from jax.sharding import PartitionSpec as P

DH = 128
F32 = jnp.float32
BF16 = jnp.bfloat16
LEFT = (((0,), (0,)), ((), ()))
RIGHT = (((1,), (1,)), ((), ()))
PLAIN = (((1,), (0,)), ((), ()))
MIB = 1024 * 1024
SIDE = 4
PAIR = 2
COLS = PAIR * DH
Q, G, K, V = range(4)

VMEM = pl.BlockSpec(memory_space=pltpu.VMEM)
HBM = pl.BlockSpec(memory_space=pltpu.HBM)
ANY = pl.BlockSpec(memory_space=pl.ANY)


def dot(a, b, dims):
    return lax.dot_general(a, b, dims, preferred_element_type=F32)


def call(body, out_shape, in_specs, out_specs, scratch=(), flops=0, nbytes=0, name=None, limit=8, **kw):
    return pl.pallas_call(
        body,
        in_specs=in_specs,
        out_specs=out_specs,
        out_shape=out_shape,
        scratch_shapes=list(scratch),
        compiler_params=pltpu.CompilerParams(vmem_limit_bytes=limit * MIB),
        cost_estimate=pl.CostEstimate(flops=flops, bytes_accessed=nbytes, transcendentals=0),
        name=name,
        **kw,
    )


def hbm(x):
    return pltpu.with_memory_space_constraint(x, pltpu.HBM)


def aligned(i, size):
    return pl.ds(pl.multiple_of(i * size, size), size)


def ring(i):
    return lax.rem(i + 2 * SIDE, SIDE)


def position():
    index = lax.axis_index("seq")
    return lax.rem(index, 2), lax.div(index, 2 * SIDE), lax.rem(lax.div(index, 2), SIDE)


def own_states(factor, act, out, side, i):
    for j in range(PAIR):
        cols = aligned((side * SIDE + i) * PAIR + j, DH)
        rows = pl.ds(j * DH, DH)
        out[i, 0, rows] = factor * dot(act[K, :, cols], act[V, :, cols], LEFT)
        out[i, 1, rows] = factor * dot(act[Q, :, cols], act[G, :, cols], LEFT)


def send_body(factor, q, g, k, v, out, act, sems):
    mine = position()[0]

    def copies(h, i):
        cols = aligned(h * SIDE + i, COLS)
        return [
            pltpu.make_async_copy(src.at[:, cols], act.at[a, :, cols], sems.at[a, h * SIDE + i])
            for a, src in enumerate((q, g, k, v))
        ]

    for h in (1 - mine, mine):
        for i in range(SIDE):
            for copy in copies(h, i):
                copy.start()

    @pl.loop(0, SIDE)
    def _(i):
        for copy in copies(1 - mine, i):
            copy.wait()
        own_states(factor, act, out, 1 - mine, i)

    for i in range(SIDE):
        for copy in copies(mine, i):
            copy.wait()


def send_states(acts, factor):
    tok, width = acts[0].shape
    return call(
        functools.partial(send_body, factor),
        [jax.ShapeDtypeStruct((SIDE, 2, COLS, DH), F32), jax.ShapeDtypeStruct((4, tok, width), BF16)],
        [HBM] * 4,
        [VMEM] * 2,
        [pltpu.SemaphoreType.DMA((4, width // COLS))],
        flops=2 * width * tok * DH,
        nbytes=8 * tok * width,
        name="send_states",
    )(*map(hbm, acts))


def keep_body(factor, act, out):
    mine = position()[0]
    for i in range(SIDE):
        own_states(factor, act, out, mine, i)


def keep_states(act, factor):
    _, tok, width = act.shape
    return call(
        functools.partial(keep_body, factor),
        jax.ShapeDtypeStruct((SIDE, 2, COLS, DH), F32),
        [VMEM],
        VMEM,
        flops=2 * width * tok * DH,
        nbytes=4 * tok * width,
        name="keep_states",
    )(act)


def split(d):
    return ((0,), (1,)) if d == 2 else ((0, 1),)


SLOTS = [(d, kinds) for d in range(SIDE) for kinds in split(d)]


def pack(out, kinds, make):
    if len(kinds) == 2:
        for kind in kinds:
            out[kind] = make(kind)
    else:
        out[...] = make(kinds[0])


def unpack(piece, kinds, kind):
    return piece[kind] if len(kinds) == 2 else piece[...]


def piece_shapes(shape):
    return [jax.ShapeDtypeStruct(shape if len(kinds) == 2 else shape[1:], F32) for _, kinds in SLOTS]


def chip_body(kept, received, *outs):
    _, _, y = position()
    for (d, kinds), out in zip(SLOTS, outs):
        s = ring(y + d)
        pack(out, kinds, lambda kind: kept[s, kind] + received[s, kind])


def chip_states(kept, received):
    return call(
        chip_body,
        piece_shapes(kept.shape[1:]),
        [VMEM] * 2,
        [VMEM] * len(SLOTS),
        flops=kept.size,
        nbytes=kept.size * 12,
        name="chip_states",
    )(kept, received)


def row_body(after, *refs):
    _, x, y = position()
    pieces, (pre, *outs), buf = refs[: len(SLOTS)], refs[len(SLOTS) : -1], refs[-1]
    for (d, kinds), piece in zip(SLOTS, pieces):
        s = ring(y - d)
        for kind in kinds:
            buf[s, kind] = unpack(piece, kinds, kind)
    ahead = jnp.zeros(buf.shape[2:], F32)
    behind = ahead
    for s in range(SIDE):
        pre[s, 0] = ahead
        ahead = ahead + buf[s, 0]
    for s in range(SIDE - 1, -1, -1):
        pre[s, 1] = behind
        behind = behind + buf[s, 1]
    for d, out in enumerate(outs, 1):
        out[...] = jnp.where(x + d < SIDE, ahead, behind)


def row_states(after, pieces):
    shape = pieces[0].shape
    return call(
        row_body,
        [jax.ShapeDtypeStruct((SIDE,) + shape, F32)] + [jax.ShapeDtypeStruct(shape[1:], F32)] * (SIDE - 1),
        [ANY] + [VMEM] * len(SLOTS),
        [VMEM] * SIDE,
        [pltpu.VMEM((SIDE,) + shape, F32)],
        flops=8 * pieces[0].size,
        nbytes=40 * pieces[0].size,
        name="row_states",
    )(after, *pieces)


def all_body(pre, *refs):
    _, x, y = position()
    totals, outs = refs[: SIDE - 1], refs[SIDE - 1 :]
    ahead = jnp.zeros(totals[0].shape, F32)
    behind = ahead
    for d, total in enumerate(totals, 1):
        lower = x >= d
        ahead = ahead + jnp.where(lower, total[...], 0.0)
        behind = behind + jnp.where(lower, 0.0, total[...])
    for (d, kinds), out in zip(SLOTS, outs):
        s = ring(y + d)
        pack(out, kinds, lambda kind: pre[s, kind] + (behind if kind else ahead))


def all_states(pre, totals):
    return call(
        all_body,
        piece_shapes(pre.shape[1:]),
        [VMEM] * SIDE,
        [VMEM] * len(SLOTS),
        flops=2 * pre.size,
        nbytes=10 * pre.size,
        name="all_states",
    )(pre, *totals)


def gather_body(after, *refs):
    core, _, y = position()
    pieces, (kept, received, mine, send) = refs[: len(SLOTS)], refs[len(SLOTS) :]
    second = core.astype(F32)
    flags = (second, 1.0 - second)
    for (d, kinds), piece in zip(SLOTS, pieces):
        s = ring(y - d)
        for kind in kinds:
            total = unpack(piece, kinds, kind)
            send[s, kind] = total + flags[1 - kind] * kept[s, kind]
            mine[s, kind] = (total + flags[kind] * received[s, kind]).astype(BF16)


def gather_states(after, pieces, kept, received):
    return call(
        gather_body,
        [jax.ShapeDtypeStruct(kept.shape, BF16), jax.ShapeDtypeStruct(kept.shape, F32)],
        [ANY] + [VMEM] * (len(SLOTS) + 2),
        [VMEM] * 2,
        flops=4 * kept.size,
        nbytes=22 * kept.size,
        name="gather_states",
    )(after, *pieces, kept, received)


def local_body(factor, first, count, after, act, *rest):
    out, tail = rest[-2:]
    tok = act.shape[1]
    causal = lax.broadcasted_iota(jnp.int32, (tok, tok), 0) >= lax.broadcasted_iota(
        jnp.int32, (tok, tok), 1
    )

    @pl.loop(first // PAIR, (first + count) // PAIR)
    def _(i):
        for j in range(PAIR):
            cols = aligned(i * PAIR + j, DH)
            qh, gh, kh, vh = (act[a, :, cols] for a in range(4))
            p = jnp.where(causal, factor * dot(qh, kh, RIGHT), 0.0).astype(BF16)
            e = jnp.where(causal, factor * dot(gh, vh, RIGHT), 0.0).astype(BF16)
            out[Q, :, cols] = dot(p, vh, PLAIN)
            out[G, :, cols] = dot(e, kh, PLAIN)
            out[K, :, cols] = dot(p, gh, LEFT)
            out[V, :, cols] = dot(e, qh, LEFT)

    tail[...] = jnp.zeros(tail.shape, F32)


def local(after, act, factor, first, count, loc=None):
    _, tok, width = act.shape
    args = [after, act]
    aliases = {}
    if loc is not None:
        args.append(loc)
        aliases = {2: 0}
    return call(
        functools.partial(local_body, factor, first, count),
        [jax.ShapeDtypeStruct((4, tok, width), F32), jax.ShapeDtypeStruct((8, DH), F32)],
        [ANY] + [VMEM] * (len(args) - 1),
        [VMEM] * 2,
        flops=12 * tok * tok * DH * count,
        nbytes=tok * width * 12,
        name="local",
        input_output_aliases=aliases,
    )(*args)


def products(side, i, state, act, loc, out):
    for j in range(PAIR):
        cols = aligned((side * SIDE + i) * PAIR + j, DH)
        here = pl.ds(j * DH, DH)
        s = state[i, 0, here].astype(BF16)
        r = state[i, 1, here].astype(BF16)
        for a, (m, dims) in enumerate(((s, PLAIN), (s, RIGHT), (r, PLAIN), (r, RIGHT))):
            out[a, i, :, here] = (loc[a, :, cols] + dot(act[a, :, cols], m, dims)).astype(BF16)


def first_body(state, act, loc, out):
    core = position()[0]

    @pl.loop(0, SIDE)
    def _(i):
        products(core, i, state, act, loc, out)


def finish_first(state, act, loc):
    _, tok, width = act.shape
    return call(
        first_body,
        jax.ShapeDtypeStruct((4, SIDE, tok, COLS), BF16),
        [VMEM] * 3,
        VMEM,
        flops=4 * tok * DH * width,
        nbytes=tok * width * 12,
        name="finish_first",
    )(state, act, loc)


def last_body(state, act, loc, first, *rest):
    outs, (buf, sems) = rest[:4], rest[4:]
    core = position()[0]

    def stores(src, h, side, i):
        cols = aligned(side * SIDE + i, COLS)
        return [pltpu.make_async_copy(src.at[a, i], out.at[:, cols], sems.at[h, a, i]) for a, out in enumerate(outs)]

    for i in range(SIDE):
        for copy in stores(first, 0, core, i):
            copy.start()

    @pl.loop(0, SIDE)
    def _(i):
        products(1 - core, i, state, act, loc, buf)
        for copy in stores(buf, 1, 1 - core, i):
            copy.start()

    for i in range(SIDE):
        for copy in stores(first, 0, core, i) + stores(buf, 1, 1 - core, i):
            copy.wait()


def finish_last(state, act, loc, first):
    _, tok, width = act.shape
    return call(
        last_body,
        [pltpu.HBM((tok, width), BF16)] * 4,
        [VMEM] * 4,
        [HBM] * 4,
        [pltpu.VMEM((4, SIDE, tok, COLS), BF16), pltpu.SemaphoreType.DMA((2, 4, SIDE))],
        flops=4 * tok * DH * width,
        nbytes=tok * width * 20,
        name="finish_last",
    )(state, act, loc, first)


def per_device(q, k, v, g):
    tok, width = q.shape
    heads = width // DH
    n = lax.axis_size("seq")
    factor = float(DH * tok * n) ** (-0.5)
    def to_sibling(t):
        return lax.ppermute(t, "seq", [(i, i ^ 1) for i in range(n)])

    def along_x(t, d):
        return lax.ppermute(t, "seq", [(i, (i + d * 2 * SIDE) % n) for i in range(n)])

    def along_y(t, d):
        row = 2 * SIDE
        return lax.ppermute(t, "seq", [(i, i // row * row + (i + 2 * d) % row) for i in range(n)])

    def gather(pieces):
        one, two, round_one, three = pieces[1:]
        by = along_y(round_one, 1)
        two = along_y(two, 2)
        one = along_y(one, 1)
        three = along_y(three, 3)
        return [pieces[0], one, two, along_y(by, 1), three]

    sent, act = send_states((q, g, k, v), factor)
    received = to_sibling(sent)
    kept = keep_states(act, factor)
    pieces = chip_states(kept, received)
    gathered = gather(pieces)
    loc, after = local(pieces[0], act, factor, 0, heads // 2)
    pre, *totals = row_states(after, gathered)
    totals = [along_x(t, d) for d, t in enumerate(totals, 1)]
    pieces = all_states(pre, totals)
    back = gather(pieces)
    loc, after = local(pieces[0], act, factor, heads // 2, heads // 2, loc)
    state, send = gather_states(after, back, kept, received)
    got = to_sibling(send)
    first = finish_first(state, act, loc)
    o, gq, gv, gk = finish_last(got, act, loc, first)
    return o, gq, gk, gv


def solution(mesh):
    placed = P(("dp", "seq"), None)
    return jax.shard_map(
        per_device,
        mesh=mesh,
        in_specs=(placed,) * 4,
        out_specs=(placed,) * 4,
        check_vma=False,
    )
```

```python
import functools

import jax
import jax.numpy as jnp
from jax import lax
from jax.experimental import pallas as pl
from jax.experimental.pallas import tpu as pltpu
from jax.sharding import PartitionSpec as P

DH = 128
F32 = jnp.float32
BF16 = jnp.bfloat16
LEFT = (((0,), (0,)), ((), ()))
RIGHT = (((1,), (1,)), ((), ()))
PLAIN = (((1,), (0,)), ((), ()))
MIB = 1024 * 1024
SIDE = 4
PAIR = 2
COLS = PAIR * DH
Q, G, K, V = range(4)
HOPS = (1, 3, 2)

VMEM = pl.BlockSpec(memory_space=pltpu.VMEM)
HBM = pl.BlockSpec(memory_space=pltpu.HBM)
ANY = pl.BlockSpec(memory_space=pl.ANY)


def dot(a, b, dims):
    return lax.dot_general(a, b, dims, preferred_element_type=F32)


def call(body, out_shape, in_specs, out_specs, scratch=(), flops=0, nbytes=0, name=None, limit=8, **kw):
    return pl.pallas_call(
        body,
        in_specs=in_specs,
        out_specs=out_specs,
        out_shape=out_shape,
        scratch_shapes=list(scratch),
        compiler_params=pltpu.CompilerParams(vmem_limit_bytes=limit * MIB),
        cost_estimate=pl.CostEstimate(flops=flops, bytes_accessed=nbytes, transcendentals=0),
        name=name,
        **kw,
    )


def hbm(x):
    return pltpu.with_memory_space_constraint(x, pltpu.HBM)


def aligned(i, size):
    return pl.ds(pl.multiple_of(i * size, size), size)


def ring(i):
    return lax.rem(i + 2 * SIDE, SIDE)


def position():
    index = lax.axis_index("seq")
    return lax.rem(index, 2), lax.div(index, 2 * SIDE), lax.rem(lax.div(index, 2), SIDE)


def own_states(factor, act, out, side, i):
    for j in range(PAIR):
        cols = aligned((side * SIDE + i) * PAIR + j, DH)
        rows = pl.ds(j * DH, DH)
        out[i, 0, rows] = factor * dot(act[K, :, cols], act[V, :, cols], LEFT)
        out[i, 1, rows] = factor * dot(act[Q, :, cols], act[G, :, cols], LEFT)


def send_body(factor, q, g, k, v, out, act, sems):
    mine = position()[0]

    def copies(h, i):
        cols = aligned(h * SIDE + i, COLS)
        return [
            pltpu.make_async_copy(src.at[:, cols], act.at[a, :, cols], sems.at[a, h * SIDE + i])
            for a, src in enumerate((q, g, k, v))
        ]

    for h in (1 - mine, mine):
        for i in range(SIDE):
            for copy in copies(h, i):
                copy.start()

    @pl.loop(0, SIDE)
    def _(i):
        for copy in copies(1 - mine, i):
            copy.wait()
        own_states(factor, act, out, 1 - mine, i)

    for i in range(SIDE):
        for copy in copies(mine, i):
            copy.wait()


def send_states(acts, factor):
    tok, width = acts[0].shape
    return call(
        functools.partial(send_body, factor),
        [jax.ShapeDtypeStruct((SIDE, 2, COLS, DH), F32), jax.ShapeDtypeStruct((4, tok, width), BF16)],
        [HBM] * 4,
        [VMEM] * 2,
        [pltpu.SemaphoreType.DMA((4, width // COLS))],
        flops=2 * width * tok * DH,
        nbytes=8 * tok * width,
        name="send_states",
    )(*map(hbm, acts))


def keep_body(factor, act, out):
    mine = position()[0]
    for i in range(SIDE):
        own_states(factor, act, out, mine, i)


def keep_states(act, factor):
    _, tok, width = act.shape
    return call(
        functools.partial(keep_body, factor),
        jax.ShapeDtypeStruct((SIDE, 2, COLS, DH), F32),
        [VMEM],
        VMEM,
        flops=2 * width * tok * DH,
        nbytes=4 * tok * width,
        name="keep_states",
    )(act)


def chip_body(kept, received, *outs):
    _, _, y = position()
    for d, out in enumerate(outs):
        s = ring(y + d)
        out[...] = kept[s] + received[s]


def chip_states(kept, received):
    return call(
        chip_body,
        [jax.ShapeDtypeStruct(kept.shape[1:], F32)] * SIDE,
        [VMEM] * 2,
        [VMEM] * SIDE,
        flops=kept.size,
        nbytes=kept.size * 12,
        name="chip_states",
    )(kept, received)


def row_body(after, *refs):
    _, x, y = position()
    pieces, (pre, *outs), buf = refs[:SIDE], refs[SIDE:-1], refs[-1]
    for d, piece in zip((0,) + HOPS, pieces):
        buf[ring(y - d)] = piece[...]
    ahead = jnp.zeros(buf.shape[2:], F32)
    behind = ahead
    for s in range(SIDE):
        pre[s, 0] = ahead
        ahead = ahead + buf[s, 0]
    for s in range(SIDE - 1, -1, -1):
        pre[s, 1] = behind
        behind = behind + buf[s, 1]
    for d, out in enumerate(outs, 1):
        out[...] = jnp.where(x + d < SIDE, ahead, behind)


def row_states(after, pieces):
    shape = pieces[0].shape
    return call(
        row_body,
        [jax.ShapeDtypeStruct((SIDE,) + shape, F32)] + [jax.ShapeDtypeStruct(shape[1:], F32)] * (SIDE - 1),
        [ANY] + [VMEM] * SIDE,
        [VMEM] * SIDE,
        [pltpu.VMEM((SIDE,) + shape, F32)],
        flops=8 * pieces[0].size,
        nbytes=40 * pieces[0].size,
        name="row_states",
    )(after, *pieces)


def all_body(pre, *refs):
    _, x, y = position()
    totals, outs = refs[: SIDE - 1], refs[SIDE - 1 :]
    ahead = jnp.zeros(totals[0].shape, F32)
    behind = ahead
    for d, total in zip(HOPS, totals):
        lower = x >= d
        ahead = ahead + jnp.where(lower, total[...], 0.0)
        behind = behind + jnp.where(lower, 0.0, total[...])
    for d, out in enumerate(outs):
        s = ring(y + d)
        out[0] = pre[s, 0] + ahead
        out[1] = pre[s, 1] + behind


def all_states(pre, totals):
    return call(
        all_body,
        [jax.ShapeDtypeStruct(pre.shape[1:], F32)] * SIDE,
        [VMEM] * SIDE,
        [VMEM] * SIDE,
        flops=2 * pre.size,
        nbytes=10 * pre.size,
        name="all_states",
    )(pre, *totals)


def gather_body(hops, after, *refs):
    count = len(hops)
    core, _, y = position()
    pieces, (kept, received, mine, send) = refs[:count], refs[count:]
    second = core.astype(F32)
    first = 1.0 - second
    for i, (d, piece) in enumerate(zip(hops, pieces)):
        s = ring(y - d)
        send[i, 0] = piece[0] + first * kept[s, 0]
        send[i, 1] = piece[1] + second * kept[s, 1]
        mine[i, 0] = (piece[0] + second * received[s, 0]).astype(BF16)
        mine[i, 1] = (piece[1] + first * received[s, 1]).astype(BF16)


def gather_states(hops, after, pieces, kept, received):
    shape = (len(hops),) + kept.shape[1:]
    size = len(hops) * pieces[0].size
    return call(
        functools.partial(gather_body, hops),
        [jax.ShapeDtypeStruct(shape, BF16), jax.ShapeDtypeStruct(shape, F32)],
        [HBM] + [VMEM] * (len(hops) + 2),
        [VMEM] * 2,
        flops=4 * size,
        nbytes=22 * size,
        name="gather_states",
    )(hbm(after), *pieces, kept, received)


def local_body(factor, first, count, after, act, *rest):
    out, tail = rest[-2:]
    tok = act.shape[1]
    causal = lax.broadcasted_iota(jnp.int32, (tok, tok), 0) >= lax.broadcasted_iota(
        jnp.int32, (tok, tok), 1
    )

    @pl.loop(first // PAIR, (first + count) // PAIR)
    def _(i):
        for j in range(PAIR):
            cols = aligned(i * PAIR + j, DH)
            qh, gh, kh, vh = (act[a, :, cols] for a in range(4))
            p = jnp.where(causal, factor * dot(qh, kh, RIGHT), 0.0).astype(BF16)
            e = jnp.where(causal, factor * dot(gh, vh, RIGHT), 0.0).astype(BF16)
            out[Q, :, cols] = dot(p, vh, PLAIN)
            out[G, :, cols] = dot(e, kh, PLAIN)
            out[K, :, cols] = dot(p, gh, LEFT)
            out[V, :, cols] = dot(e, qh, LEFT)

    tail[...] = jnp.zeros(tail.shape, F32)


def local(after, act, factor, first, count, loc=None):
    _, tok, width = act.shape
    args = [after, act]
    aliases = {}
    if loc is not None:
        args.append(loc)
        aliases = {2: 0}
    return call(
        functools.partial(local_body, factor, first, count),
        [jax.ShapeDtypeStruct((4, tok, width), F32), jax.ShapeDtypeStruct((8, DH), F32)],
        [ANY] + [VMEM] * (len(args) - 1),
        [VMEM] * 2,
        flops=12 * tok * tok * DH * count,
        nbytes=tok * width * 12,
        name="local",
        input_output_aliases=aliases,
    )(*args)


def finish_body(hops, own, state, act, loc, *rest):
    *outs, obuf, sems = rest[-6:]
    core, _, y = position()
    side = core if own else 1 - core

    def place(i):
        hop = lax.rem(2 * i, SIDE - 1) + 1 if len(hops) > 1 else 0
        return (side * SIDE + ring(y - hop)) * PAIR

    def stores(i):
        cols = pl.ds(pl.multiple_of(place(i) * DH, COLS), COLS)
        return [pltpu.make_async_copy(obuf.at[a, i], out.at[:, cols], sems.at[a, i]) for a, out in enumerate(outs)]

    @pl.loop(0, len(hops))
    def _(i):
        for j in range(PAIR):
            cols = aligned(place(i) + j, DH)
            here = pl.ds(j * DH, DH)
            s = state[i, 0, here].astype(BF16)
            r = state[i, 1, here].astype(BF16)
            for a, (m, dims) in enumerate(((s, PLAIN), (s, RIGHT), (r, PLAIN), (r, RIGHT))):
                obuf[a, i, :, here] = (loc[a, :, cols] + dot(act[a, :, cols], m, dims)).astype(BF16)
        for copy in stores(i):
            copy.start()

    for i in range(len(hops)):
        for copy in stores(i):
            copy.wait()


def finish(hops, own, state, act, loc, outs):
    _, tok, width = act.shape
    args = [state, act, loc]
    specs = [VMEM] * 3
    aliases = {}
    if outs is not None:
        aliases = {len(args) + i: i for i in range(4)}
        args += map(hbm, outs)
        specs += [HBM] * 4
    return call(
        functools.partial(finish_body, hops, own),
        [pltpu.HBM((tok, width), BF16)] * 4,
        specs,
        [HBM] * 4,
        [pltpu.VMEM((4, len(hops), tok, COLS), BF16), pltpu.SemaphoreType.DMA((4, len(hops)))],
        flops=len(hops) * tok * DH * width,
        nbytes=len(hops) * tok * width * 4,
        name="finish",
        input_output_aliases=aliases,
    )(*args)


def per_device(q, k, v, g):
    tok, width = q.shape
    heads = width // DH
    n = lax.axis_size("seq")
    factor = float(DH * tok * n) ** (-0.5)
    def to_sibling(t):
        return lax.ppermute(t, "seq", [(i, i ^ 1) for i in range(n)])

    def along_x(t, d):
        return lax.ppermute(t, "seq", [(i, (i + d * 2 * SIDE) % n) for i in range(n)])

    def along_y(t, d):
        row = 2 * SIDE
        return lax.ppermute(t, "seq", [(i, i // row * row + (i + 2 * d) % row) for i in range(n)])

    sent, act = send_states((q, g, k, v), factor)
    received = to_sibling(sent)
    kept = keep_states(act, factor)
    pieces = chip_states(kept, received)
    gathered = {0: pieces[0]}
    for d in HOPS:
        gathered[d] = along_y(pieces[d], d)
    loc, after = local(pieces[0], act, factor, 0, heads)
    pre, *sums = row_states(after, [gathered[d] for d in (0,) + HOPS])
    totals = {}
    for d in HOPS:
        totals[d] = along_x(sums[d - 1], d)
    pieces = all_states(pre, [totals[d] for d in HOPS])
    back = {0: pieces[0]}
    for d in HOPS:
        back[d] = along_y(pieces[d], d)
    outs, after = None, q
    for hops in ((0,), HOPS):
        state, send = gather_states(hops, after, [back[d] for d in hops], kept, received)
        got = to_sibling(send)
        outs = finish(hops, True, state, act, loc, outs)
        outs = finish(hops, False, got, act, loc, outs)
        after = outs[0]
    o, gq, gv, gk = outs
    return o, gq, gk, gv


def solution(mesh):
    placed = P(("dp", "seq"), None)
    return jax.shard_map(
        per_device,
        mesh=mesh,
        in_specs=(placed,) * 4,
        out_specs=(placed,) * 4,
        check_vma=False,
    )
```

```python
import functools

import jax
import jax.numpy as jnp
from jax import lax
from jax.experimental import pallas as pl
from jax.experimental.pallas import tpu as pltpu
from jax.sharding import PartitionSpec as P

DH = 128
F32 = jnp.float32
BF16 = jnp.bfloat16
LEFT = (((0,), (0,)), ((), ()))
RIGHT = (((1,), (1,)), ((), ()))
PLAIN = (((1,), (0,)), ((), ()))
MIB = 1024 * 1024
SIDE = 4
PAIR = 2
COLS = PAIR * DH
Q, G, K, V = range(4)
HOPS = (1, 3, 2)

VMEM = pl.BlockSpec(memory_space=pltpu.VMEM)
HBM = pl.BlockSpec(memory_space=pltpu.HBM)
ANY = pl.BlockSpec(memory_space=pl.ANY)


def dot(a, b, dims):
    return lax.dot_general(a, b, dims, preferred_element_type=F32)


def call(body, out_shape, in_specs, out_specs, scratch=(), flops=0, nbytes=0, name=None, limit=8, **kw):
    return pl.pallas_call(
        body,
        in_specs=in_specs,
        out_specs=out_specs,
        out_shape=out_shape,
        scratch_shapes=list(scratch),
        compiler_params=pltpu.CompilerParams(vmem_limit_bytes=limit * MIB),
        cost_estimate=pl.CostEstimate(flops=flops, bytes_accessed=nbytes, transcendentals=0),
        name=name,
        **kw,
    )


def hbm(x):
    return pltpu.with_memory_space_constraint(x, pltpu.HBM)


def aligned(i, size):
    return pl.ds(pl.multiple_of(i * size, size), size)


def ring(i):
    return lax.rem(i + 2 * SIDE, SIDE)


def position():
    index = lax.axis_index("seq")
    return lax.rem(index, 2), lax.div(index, 2 * SIDE), lax.rem(lax.div(index, 2), SIDE)


def own_states(factor, act, out, side, i):
    for j in range(PAIR):
        cols = aligned((side * SIDE + i) * PAIR + j, DH)
        rows = pl.ds(j * DH, DH)
        out[i, 0, rows] = factor * dot(act[K, :, cols], act[V, :, cols], LEFT)
        out[i, 1, rows] = factor * dot(act[Q, :, cols], act[G, :, cols], LEFT)


def send_body(factor, q, g, k, v, out, act, sems):
    mine = position()[0]

    def copies(h, i):
        cols = aligned(h * SIDE + i, COLS)
        return [
            pltpu.make_async_copy(src.at[:, cols], act.at[a, :, cols], sems.at[a, h * SIDE + i])
            for a, src in enumerate((q, g, k, v))
        ]

    for h in (1 - mine, mine):
        for i in range(SIDE):
            for copy in copies(h, i):
                copy.start()

    @pl.loop(0, SIDE)
    def _(i):
        for copy in copies(1 - mine, i):
            copy.wait()
        own_states(factor, act, out, 1 - mine, i)

    for i in range(SIDE):
        for copy in copies(mine, i):
            copy.wait()


def send_states(acts, factor):
    tok, width = acts[0].shape
    return call(
        functools.partial(send_body, factor),
        [jax.ShapeDtypeStruct((SIDE, 2, COLS, DH), F32), jax.ShapeDtypeStruct((4, tok, width), BF16)],
        [HBM] * 4,
        [VMEM] * 2,
        [pltpu.SemaphoreType.DMA((4, width // COLS))],
        flops=2 * width * tok * DH,
        nbytes=8 * tok * width,
        name="send_states",
    )(*map(hbm, acts))


def keep_body(factor, act, out):
    mine = position()[0]
    for i in range(SIDE):
        own_states(factor, act, out, mine, i)


def keep_states(act, factor):
    _, tok, width = act.shape
    return call(
        functools.partial(keep_body, factor),
        jax.ShapeDtypeStruct((SIDE, 2, COLS, DH), F32),
        [VMEM],
        VMEM,
        flops=2 * width * tok * DH,
        nbytes=4 * tok * width,
        name="keep_states",
    )(act)


def chip_body(kept, received, *outs):
    _, _, y = position()
    for d, out in enumerate(outs):
        s = ring(y + d)
        out[...] = kept[s] + received[s]


def chip_states(kept, received):
    return call(
        chip_body,
        [jax.ShapeDtypeStruct(kept.shape[1:], F32)] * SIDE,
        [VMEM] * 2,
        [VMEM] * SIDE,
        flops=kept.size,
        nbytes=kept.size * 12,
        name="chip_states",
    )(kept, received)


def row_body(after, *refs):
    _, x, y = position()
    pieces, (pre, *outs), buf = refs[:SIDE], refs[SIDE:-1], refs[-1]
    for d, piece in zip((0,) + HOPS, pieces):
        buf[ring(y - d)] = piece[...]
    ahead = jnp.zeros(buf.shape[2:], F32)
    behind = ahead
    for s in range(SIDE):
        pre[s, 0] = ahead
        ahead = ahead + buf[s, 0]
    for s in range(SIDE - 1, -1, -1):
        pre[s, 1] = behind
        behind = behind + buf[s, 1]
    for d, out in enumerate(outs, 1):
        out[...] = jnp.where(x + d < SIDE, ahead, behind)


def row_states(after, pieces):
    shape = pieces[0].shape
    return call(
        row_body,
        [jax.ShapeDtypeStruct((SIDE,) + shape, F32)] + [jax.ShapeDtypeStruct(shape[1:], F32)] * (SIDE - 1),
        [ANY] + [VMEM] * SIDE,
        [VMEM] * SIDE,
        [pltpu.VMEM((SIDE,) + shape, F32)],
        flops=8 * pieces[0].size,
        nbytes=40 * pieces[0].size,
        name="row_states",
    )(after, *pieces)


def all_body(pre, *refs):
    _, x, y = position()
    totals, outs = refs[: SIDE - 1], refs[SIDE - 1 :]
    ahead = jnp.zeros(totals[0].shape, F32)
    behind = ahead
    for d, total in zip(HOPS, totals):
        lower = x >= d
        ahead = ahead + jnp.where(lower, total[...], 0.0)
        behind = behind + jnp.where(lower, 0.0, total[...])
    for d, out in enumerate(outs):
        s = ring(y + d)
        out[0] = pre[s, 0] + ahead
        out[1] = pre[s, 1] + behind


def all_states(pre, totals):
    return call(
        all_body,
        [jax.ShapeDtypeStruct(pre.shape[1:], F32)] * SIDE,
        [VMEM] * SIDE,
        [VMEM] * SIDE,
        flops=2 * pre.size,
        nbytes=10 * pre.size,
        name="all_states",
    )(pre, *totals)


def gather_body(after, *refs):
    core, _, y = position()
    pieces, (kept, received, mine, send) = refs[:SIDE], refs[SIDE:]
    second = core.astype(F32)
    first = 1.0 - second
    for d, piece in zip((0,) + HOPS, pieces):
        s = ring(y - d)
        send[s, 0] = piece[0] + first * kept[s, 0]
        send[s, 1] = piece[1] + second * kept[s, 1]
        mine[s, 0] = (piece[0] + second * received[s, 0]).astype(BF16)
        mine[s, 1] = (piece[1] + first * received[s, 1]).astype(BF16)


def gather_states(after, pieces, kept, received):
    return call(
        gather_body,
        [jax.ShapeDtypeStruct(kept.shape, BF16), jax.ShapeDtypeStruct(kept.shape, F32)],
        [ANY] + [VMEM] * (SIDE + 2),
        [VMEM] * 2,
        flops=4 * kept.size,
        nbytes=22 * kept.size,
        name="gather_states",
    )(after, *pieces, kept, received)


def local_body(factor, first, count, after, act, *rest):
    out, tail = rest[-2:]
    tok = act.shape[1]
    causal = lax.broadcasted_iota(jnp.int32, (tok, tok), 0) >= lax.broadcasted_iota(
        jnp.int32, (tok, tok), 1
    )

    @pl.loop(first // PAIR, (first + count) // PAIR)
    def _(i):
        for j in range(PAIR):
            cols = aligned(i * PAIR + j, DH)
            qh, gh, kh, vh = (act[a, :, cols] for a in range(4))
            p = jnp.where(causal, factor * dot(qh, kh, RIGHT), 0.0).astype(BF16)
            e = jnp.where(causal, factor * dot(gh, vh, RIGHT), 0.0).astype(BF16)
            out[Q, :, cols] = dot(p, vh, PLAIN)
            out[G, :, cols] = dot(e, kh, PLAIN)
            out[K, :, cols] = dot(p, gh, LEFT)
            out[V, :, cols] = dot(e, qh, LEFT)

    tail[...] = jnp.zeros(tail.shape, F32)


def local(after, act, factor, first, count, loc=None):
    _, tok, width = act.shape
    args = [after, act]
    aliases = {}
    if loc is not None:
        args.append(loc)
        aliases = {2: 0}
    return call(
        functools.partial(local_body, factor, first, count),
        [jax.ShapeDtypeStruct((4, tok, width), F32), jax.ShapeDtypeStruct((8, DH), F32)],
        [ANY] + [VMEM] * (len(args) - 1),
        [VMEM] * 2,
        flops=12 * tok * tok * DH * count,
        nbytes=tok * width * 12,
        name="local",
        input_output_aliases=aliases,
    )(*args)


def finish_body(own, state, act, loc, *rest):
    outs, (obuf, sems) = rest[-6:-2], rest[-2:]
    core = position()[0]
    side = core if own else 1 - core

    def stores(i):
        return [
            pltpu.make_async_copy(
                obuf.at[a, :, aligned(i, COLS)], out.at[:, aligned(side * SIDE + i, COLS)], sems.at[a, i]
            )
            for a, out in enumerate(outs)
        ]

    @pl.loop(0, SIDE)
    def _(i):
        for j in range(PAIR):
            cols = aligned((side * SIDE + i) * PAIR + j, DH)
            here = aligned(i * PAIR + j, DH)
            rows = pl.ds(j * DH, DH)
            s = state[i, 0, rows].astype(BF16)
            r = state[i, 1, rows].astype(BF16)
            for a, (m, dims) in enumerate(((s, PLAIN), (s, RIGHT), (r, PLAIN), (r, RIGHT))):
                obuf[a, :, here] = (loc[a, :, cols] + dot(act[a, :, cols], m, dims)).astype(BF16)
        for copy in stores(i):
            copy.start()

    for i in range(SIDE):
        for copy in stores(i):
            copy.wait()


def finish(state, act, loc, outs=None):
    _, tok, width = act.shape
    args = [state, act, loc]
    specs = [VMEM] * 3
    aliases = {}
    if outs is not None:
        aliases = {len(args) + i: i for i in range(4)}
        args += map(hbm, outs)
        specs += [HBM] * 4
    return call(
        functools.partial(finish_body, outs is None),
        [pltpu.HBM((tok, width), BF16)] * 4,
        specs,
        [HBM] * 4,
        [pltpu.VMEM((4, tok, width // 2), BF16), pltpu.SemaphoreType.DMA((4, SIDE))],
        flops=4 * tok * DH * width,
        nbytes=tok * width * 16,
        name="finish",
        input_output_aliases=aliases,
    )(*args)


def per_device(q, k, v, g):
    tok, width = q.shape
    heads = width // DH
    n = lax.axis_size("seq")
    factor = float(DH * tok * n) ** (-0.5)
    def to_sibling(t):
        return lax.ppermute(t, "seq", [(i, i ^ 1) for i in range(n)])

    def along_x(t, d):
        return lax.ppermute(t, "seq", [(i, (i + d * 2 * SIDE) % n) for i in range(n)])

    def along_y(t, d):
        row = 2 * SIDE
        return lax.ppermute(t, "seq", [(i, i // row * row + (i + 2 * d) % row) for i in range(n)])

    sent, act = send_states((q, g, k, v), factor)
    received = to_sibling(sent)
    kept = keep_states(act, factor)
    pieces = chip_states(kept, received)
    gathered = [pieces[0]] + [along_y(pieces[d], d) for d in HOPS]
    loc, after = local(pieces[0], act, factor, 0, heads // 2)
    pre, *totals = row_states(after, gathered)
    totals = [along_x(totals[d - 1], d) for d in HOPS]
    pieces = all_states(pre, totals)
    back = [pieces[0]] + [along_y(pieces[d], d) for d in HOPS]
    loc, after = local(pieces[0], act, factor, heads // 2, heads // 2, loc)
    state, send = gather_states(after, back, kept, received)
    got = to_sibling(send)
    outs = finish(state, act, loc)
    o, gq, gv, gk = finish(got, act, loc, outs)
    return o, gq, gk, gv


def solution(mesh):
    placed = P(("dp", "seq"), None)
    return jax.shard_map(
        per_device,
        mesh=mesh,
        in_specs=(placed,) * 4,
        out_specs=(placed,) * 4,
        check_vma=False,
    )
```

```python
import functools

import jax
import jax.numpy as jnp
from jax import lax
from jax.experimental import pallas as pl
from jax.experimental.pallas import tpu as pltpu
from jax.sharding import PartitionSpec as P

DH = 128
F32 = jnp.float32
BF16 = jnp.bfloat16
LEFT = (((0,), (0,)), ((), ()))
RIGHT = (((1,), (1,)), ((), ()))
PLAIN = (((1,), (0,)), ((), ()))
MIB = 1024 * 1024
SIDE = 4
PAIR = 2
COLS = PAIR * DH
Q, G, K, V = range(4)
HOPS = (1, 3, 2)
ORDER = HOPS + (0,)
EARLY = 2

VMEM = pl.BlockSpec(memory_space=pltpu.VMEM)
HBM = pl.BlockSpec(memory_space=pltpu.HBM)
ANY = pl.BlockSpec(memory_space=pl.ANY)


def dot(a, b, dims):
    return lax.dot_general(a, b, dims, preferred_element_type=F32)


def call(body, out_shape, in_specs, out_specs, scratch=(), flops=0, nbytes=0, name=None, limit=8, **kw):
    return pl.pallas_call(
        body,
        in_specs=in_specs,
        out_specs=out_specs,
        out_shape=out_shape,
        scratch_shapes=list(scratch),
        compiler_params=pltpu.CompilerParams(vmem_limit_bytes=limit * MIB),
        cost_estimate=pl.CostEstimate(flops=flops, bytes_accessed=nbytes, transcendentals=0),
        name=name,
        **kw,
    )


def hbm(x):
    return pltpu.with_memory_space_constraint(x, pltpu.HBM)


def aligned(i, size):
    return pl.ds(pl.multiple_of(i * size, size), size)


def ring(i):
    return lax.rem(i + 2 * SIDE, SIDE)


def position():
    index = lax.axis_index("seq")
    return lax.rem(index, 2), lax.div(index, 2 * SIDE), lax.rem(lax.div(index, 2), SIDE)


def own_states(factor, act, out, slot, side, i):
    for j in range(PAIR):
        cols = aligned((side * SIDE + i) * PAIR + j, DH)
        rows = pl.ds(j * DH, DH)
        out[slot, 0, rows] = factor * dot(act[K, :, cols], act[V, :, cols], LEFT)
        out[slot, 1, rows] = factor * dot(act[Q, :, cols], act[G, :, cols], LEFT)


def send_body(factor, q, g, k, v, early, late, act, sems):
    mine, _, y = position()

    def copies(h, i):
        cols = aligned(h * SIDE + i, COLS)
        return [
            pltpu.make_async_copy(src.at[:, cols], act.at[a, :, cols], sems.at[a, h * SIDE + i])
            for a, src in enumerate((q, g, k, v))
        ]

    for h in (1 - mine, mine):
        for d in ORDER:
            for copy in copies(h, ring(y + d)):
                copy.start()
    for slot, d in enumerate(ORDER):
        i = ring(y + d)
        for copy in copies(1 - mine, i):
            copy.wait()
        out = early if slot < EARLY else late
        own_states(factor, act, out, slot % EARLY, 1 - mine, i)

    for i in range(SIDE):
        for copy in copies(mine, i):
            copy.wait()


def send_states(acts, factor):
    tok, width = acts[0].shape
    return call(
        functools.partial(send_body, factor),
        [jax.ShapeDtypeStruct((EARLY, 2, COLS, DH), F32)] * 2 + [jax.ShapeDtypeStruct((4, tok, width), BF16)],
        [HBM] * 4,
        [VMEM] * 3,
        [pltpu.SemaphoreType.DMA((4, width // COLS))],
        flops=2 * width * tok * DH,
        nbytes=8 * tok * width,
        name="send_states",
    )(*map(hbm, acts))


def keep_body(factor, act, out):
    mine, _, y = position()
    for slot, d in enumerate(ORDER):
        own_states(factor, act, out, slot, mine, ring(y + d))


def keep_states(act, factor):
    _, tok, width = act.shape
    return call(
        functools.partial(keep_body, factor),
        jax.ShapeDtypeStruct((SIDE, 2, COLS, DH), F32),
        [VMEM],
        VMEM,
        flops=2 * width * tok * DH,
        nbytes=4 * tok * width,
        name="keep_states",
    )(act)


def chip_body(first, kept, received, *outs):
    for i, out in enumerate(outs):
        out[...] = kept[first + i] + received[i]


def chip_states(first, kept, received):
    return call(
        functools.partial(chip_body, first),
        [jax.ShapeDtypeStruct(kept.shape[1:], F32)] * EARLY,
        [VMEM] * 2,
        [VMEM] * EARLY,
        flops=received.size,
        nbytes=received.size * 12,
        name="chip_states",
    )(kept, received)


def row_body(after, *refs):
    _, x, y = position()
    pieces, (pre, *outs), buf = refs[:SIDE], refs[SIDE:-1], refs[-1]
    for d, piece in zip((0,) + HOPS, pieces):
        buf[ring(y - d)] = piece[...]
    ahead = jnp.zeros(buf.shape[2:], F32)
    behind = ahead
    for s in range(SIDE):
        pre[s, 0] = ahead
        ahead = ahead + buf[s, 0]
    for s in range(SIDE - 1, -1, -1):
        pre[s, 1] = behind
        behind = behind + buf[s, 1]
    for d, out in enumerate(outs, 1):
        out[...] = jnp.where(x + d < SIDE, ahead, behind)


def row_states(after, pieces):
    shape = pieces[0].shape
    return call(
        row_body,
        [jax.ShapeDtypeStruct((SIDE,) + shape, F32)] + [jax.ShapeDtypeStruct(shape[1:], F32)] * (SIDE - 1),
        [ANY] + [VMEM] * SIDE,
        [VMEM] * SIDE,
        [pltpu.VMEM((SIDE,) + shape, F32)],
        flops=8 * pieces[0].size,
        nbytes=40 * pieces[0].size,
        name="row_states",
    )(after, *pieces)


def all_body(pre, *refs):
    _, x, y = position()
    totals, outs = refs[: SIDE - 1], refs[SIDE - 1 :]
    ahead = jnp.zeros(totals[0].shape, F32)
    behind = ahead
    for d, total in zip(HOPS, totals):
        lower = x >= d
        ahead = ahead + jnp.where(lower, total[...], 0.0)
        behind = behind + jnp.where(lower, 0.0, total[...])
    for d, out in enumerate(outs):
        s = ring(y + d)
        out[0] = pre[s, 0] + ahead
        out[1] = pre[s, 1] + behind


def all_states(pre, totals):
    return call(
        all_body,
        [jax.ShapeDtypeStruct(pre.shape[1:], F32)] * SIDE,
        [VMEM] * SIDE,
        [VMEM] * SIDE,
        flops=2 * pre.size,
        nbytes=10 * pre.size,
        name="all_states",
    )(pre, *totals)


def gather_body(after, *refs):
    core, _, y = position()
    pieces, (kept, early, late, mine, send) = refs[:SIDE], refs[SIDE:]
    second = core.astype(F32)
    first = 1.0 - second
    for d, piece in zip((0,) + HOPS, pieces):
        s = ring(y - d)
        slot = ORDER.index((SIDE - d) % SIDE)
        received = (early if slot < EARLY else late).at[slot % EARLY]
        send[s, 0] = piece[0] + first * kept[slot, 0]
        send[s, 1] = piece[1] + second * kept[slot, 1]
        mine[s, 0] = (piece[0] + second * received[0]).astype(BF16)
        mine[s, 1] = (piece[1] + first * received[1]).astype(BF16)


def gather_states(after, pieces, kept, received):
    return call(
        gather_body,
        [jax.ShapeDtypeStruct(kept.shape, BF16), jax.ShapeDtypeStruct(kept.shape, F32)],
        [ANY] + [VMEM] * (SIDE + 3),
        [VMEM] * 2,
        flops=4 * kept.size,
        nbytes=22 * kept.size,
        name="gather_states",
    )(after, *pieces, kept, *received)


def local_body(factor, first, count, after, act, *rest):
    out, tail = rest[-2:]
    tok = act.shape[1]
    causal = lax.broadcasted_iota(jnp.int32, (tok, tok), 0) >= lax.broadcasted_iota(
        jnp.int32, (tok, tok), 1
    )

    @pl.loop(first // PAIR, (first + count) // PAIR)
    def _(i):
        for j in range(PAIR):
            cols = aligned(i * PAIR + j, DH)
            qh, gh, kh, vh = (act[a, :, cols] for a in range(4))
            p = jnp.where(causal, factor * dot(qh, kh, RIGHT), 0.0).astype(BF16)
            e = jnp.where(causal, factor * dot(gh, vh, RIGHT), 0.0).astype(BF16)
            out[Q, :, cols] = dot(p, vh, PLAIN)
            out[G, :, cols] = dot(e, kh, PLAIN)
            out[K, :, cols] = dot(p, gh, LEFT)
            out[V, :, cols] = dot(e, qh, LEFT)

    tail[...] = jnp.zeros(tail.shape, F32)


def local(after, act, factor, first, count, loc=None):
    _, tok, width = act.shape
    args = [after, act]
    aliases = {}
    if loc is not None:
        args.append(loc)
        aliases = {2: 0}
    return call(
        functools.partial(local_body, factor, first, count),
        [jax.ShapeDtypeStruct((4, tok, width), F32), jax.ShapeDtypeStruct((8, DH), F32)],
        [ANY] + [VMEM] * (len(args) - 1),
        [VMEM] * 2,
        flops=12 * tok * tok * DH * count,
        nbytes=tok * width * 12,
        name="local",
        input_output_aliases=aliases,
    )(*args)


def finish_body(own, state, act, loc, *rest):
    outs, (obuf, sems) = rest[-6:-2], rest[-2:]
    core = position()[0]
    side = core if own else 1 - core

    def stores(i):
        return [
            pltpu.make_async_copy(
                obuf.at[a, :, aligned(i, COLS)], out.at[:, aligned(side * SIDE + i, COLS)], sems.at[a, i]
            )
            for a, out in enumerate(outs)
        ]

    @pl.loop(0, SIDE)
    def _(i):
        for j in range(PAIR):
            cols = aligned((side * SIDE + i) * PAIR + j, DH)
            here = aligned(i * PAIR + j, DH)
            rows = pl.ds(j * DH, DH)
            s = state[i, 0, rows].astype(BF16)
            r = state[i, 1, rows].astype(BF16)
            for a, (m, dims) in enumerate(((s, PLAIN), (s, RIGHT), (r, PLAIN), (r, RIGHT))):
                obuf[a, :, here] = (loc[a, :, cols] + dot(act[a, :, cols], m, dims)).astype(BF16)
        for copy in stores(i):
            copy.start()

    for i in range(SIDE):
        for copy in stores(i):
            copy.wait()


def finish(state, act, loc, outs=None):
    _, tok, width = act.shape
    args = [state, act, loc]
    specs = [VMEM] * 3
    aliases = {}
    if outs is not None:
        aliases = {len(args) + i: i for i in range(4)}
        args += map(hbm, outs)
        specs += [HBM] * 4
    return call(
        functools.partial(finish_body, outs is None),
        [pltpu.HBM((tok, width), BF16)] * 4,
        specs,
        [HBM] * 4,
        [pltpu.VMEM((4, tok, width // 2), BF16), pltpu.SemaphoreType.DMA((4, SIDE))],
        flops=4 * tok * DH * width,
        nbytes=tok * width * 16,
        name="finish",
        input_output_aliases=aliases,
    )(*args)


def per_device(q, k, v, g):
    tok, width = q.shape
    heads = width // DH
    n = lax.axis_size("seq")
    factor = float(DH * tok * n) ** (-0.5)
    def to_sibling(t):
        return lax.ppermute(t, "seq", [(i, i ^ 1) for i in range(n)])

    def along_x(t, d):
        return lax.ppermute(t, "seq", [(i, (i + d * 2 * SIDE) % n) for i in range(n)])

    def along_y(t, d):
        row = 2 * SIDE
        return lax.ppermute(t, "seq", [(i, i // row * row + (i + 2 * d) % row) for i in range(n)])

    *sent, act = send_states((q, g, k, v), factor)
    received = [to_sibling(t) for t in sent]
    kept = keep_states(act, factor)
    pieces = [t for i in range(2) for t in chip_states(i * EARLY, kept, received[i])]
    pieces = dict(zip(ORDER, pieces))
    gathered = [pieces[0]] + [along_y(pieces[d], d) for d in HOPS]
    loc, after = local(pieces[0], act, factor, 0, heads // 2)
    pre, *totals = row_states(after, gathered)
    totals = [along_x(totals[d - 1], d) for d in HOPS]
    pieces = all_states(pre, totals)
    back = [pieces[0]] + [along_y(pieces[d], d) for d in HOPS]
    loc, after = local(pieces[0], act, factor, heads // 2, heads // 2, loc)
    state, send = gather_states(after, back, kept, received)
    got = to_sibling(send)
    outs = finish(state, act, loc)
    o, gq, gv, gk = finish(got, act, loc, outs)
    return o, gq, gk, gv


def solution(mesh):
    placed = P(("dp", "seq"), None)
    return jax.shard_map(
        per_device,
        mesh=mesh,
        in_specs=(placed,) * 4,
        out_specs=(placed,) * 4,
        check_vma=False,
    )
```
